128 devices in a mesh: grp: 4 (over y), dev: 32 (over x, z, core).
Axes of the slice: x: 4, y: 4, z: 4, core: 2. Of those that a mesh axis runs over, the one named last changes fastest.
Arguments:
- cand_rows: bfloat16 [32768, 1024], P(('grp', 'dev'))
- cand_col: int32 [32768], P(('grp', 'dev')), may hold values from 0 to 31, as said below
- w_in: bfloat16 [1024, 4096], replicated, may hold values from -0.1875 to 0.1875
- w_out: bfloat16 [1024, 1024], replicated, may hold values from -0.1875 to 0.1875
- hist_keys: bfloat16 [4, 32, 2048, 1024], P(None, 'dev', 'grp'), may hold values from -6 to 6
- hist_vals: bfloat16 [4, 32, 2048, 1024], P(None, 'dev', 'grp'), may hold values from -0.59765625 to 0.59765625
- hist_len: int32 [4, 32], P(None, 'dev'), may hold values from 512 to 2048
Outputs:
- scored_rows: bfloat16 [32768, 1024], P(('grp', 'dev'))
The draws below stay inside these ranges and needn't reach their ends.
Inputs may be any that keep to these rules, and one draw needn't show every extreme that they name: `cand_col`: on each device, each user of its group is named by at most 32 of its rows; in every group one user is named by exactly 32 rows of every device of the group.
All inputs are finite; a program needn't handle non-finite values.
Results may differ from the reference program's by a relative error of at most 0.007.
Values may be sent and summed in bfloat16 or wider, within the bound.
A program may use at most 192 MiB of HBM per device.

```python
import math
import jax
import jax.numpy as jnp
from jax import lax

D = 1024
HEADS = 16
HEAD_WIDTH = 64
HIST = 2048
ROW_DEV = 256
MOST = 32
GROUPS = 4
COLS = 32
TOKENS = 32768


def draw_cand_rows(key, part):
    key = jax.random.fold_in(key, 5)
    noise_key, row_key, col_key = jax.random.split(key, 3)
    row_scale = jnp.exp(jax.random.uniform(row_key, (TOKENS, 1), minval=math.log(0.3), maxval=math.log(3.0)))
    col_scale = jnp.exp(jax.random.uniform(col_key, (1, D), minval=math.log(0.3), maxval=math.log(3.0)))
    noise_values = jax.random.truncated_normal(noise_key, -4.0, 4.0, (TOKENS, D))
    return (noise_values * row_scale * col_scale).astype(jnp.float32).astype(jnp.bfloat16)


def draw_cand_col(key, part):
    key = jax.random.fold_in(key, 9)
    hot_key, slot_key = jax.random.split(key, 2)
    hot_cols = jax.random.randint(hot_key, (GROUPS,), 0, COLS)
    device_keys = jax.random.split(slot_key, GROUPS * COLS)
    device_hot = jnp.repeat(hot_cols, COLS)

    def per_device(device_key, hot_col):
        first_key, second_key = jax.random.split(device_key, 2)
        slots = jax.random.permutation(first_key, (COLS - 1) * MOST)[:ROW_DEV - MOST]
        others = slots // MOST
        others = others + (others >= hot_col).astype(jnp.int32)
        columns = jnp.concatenate([jnp.full((MOST,), hot_col, dtype=jnp.int32), others.astype(jnp.int32)])
        return jax.random.permutation(second_key, columns)
    result = jax.vmap(per_device)(device_keys, device_hot)
    return result.reshape(TOKENS).astype(jnp.int32)


def draw_hist_len(key, part):
    key = jax.random.fold_in(key, 13)
    draw_key, pick_key, other_key = jax.random.split(key, 3)
    user_count = GROUPS * COLS
    lengths = jax.random.randint(draw_key, (user_count,), HIST // 4, HIST + 1)
    longest = jax.random.randint(pick_key, (), 0, user_count)
    shortest = (longest + 1 + jax.random.randint(other_key, (), 0, user_count - 1)) % user_count
    lengths = lengths.at[longest].set(HIST).at[shortest].set(HIST // 4)
    return lengths.reshape(GROUPS, COLS).astype(jnp.int32)


def level_of(key, dims, pieces, smallest, high):
    gain = 1.0
    for position, shards_of in pieces:
        draws = jax.random.uniform(jax.random.fold_in(jax.random.fold_in(key, 6), position), (shards_of,), jnp.float32, smallest / len(pieces), high / len(pieces))
        gain = gain * jnp.repeat(jnp.exp(draws), dims[position] // shards_of).reshape((-1,) + (1,) * (len(dims) - 1 - position))
    return gain


def scatter_about(stream_key, dims, spread, reach, cuts=(), kind=jnp.bfloat16):
    values = spread * jax.random.normal(stream_key, dims, jnp.float32)
    if cuts:
        values = values * level_of(stream_key, dims, cuts, -0.22, 0.18)
    return jnp.clip(values, -reach, reach).astype(kind)


def setup_inputs(seed: int = 0) -> dict:
    arg_keys = jax.random.split(jax.random.key(seed), 8)
    return {
        "cand_rows": draw_cand_rows(jax.random.fold_in(arg_keys[7], 71), 0),
        "cand_col": draw_cand_col(jax.random.fold_in(arg_keys[7], 71), 0),
        "w_in": scatter_about(arg_keys[2], (D, 4 * D), D ** -0.5, 0.1875),
        "w_out": scatter_about(arg_keys[3], (D, D), D ** -0.5, 0.1875),
        "hist_keys": scatter_about(arg_keys[4], (GROUPS, COLS, HIST, D), 1.0, 6.0, ((1, 32), (2, 4))),
        "hist_vals": scatter_about(arg_keys[5], (GROUPS, COLS, HIST, D), 0.1, 0.59765625, ((1, 32), (2, 4))),
        "hist_len": draw_hist_len(jax.random.fold_in(arg_keys[7], 71), 0),
    }


def layer_rows(values):
    row_mean = lax.optimization_barrier(jnp.mean(values, axis=-1, keepdims=True))
    centred = values - row_mean
    variance = lax.optimization_barrier(jnp.mean(centred * centred, axis=-1, keepdims=True))
    return centred / jnp.sqrt(variance + 1e-05)

def self_scores(query_part, key_part, value_part):
    row_count = query_part.shape[0]
    query_head_split = query_part.astype(jnp.float32).reshape(row_count, HEADS, HEAD_WIDTH)
    key_head_split = key_part.astype(jnp.float32).reshape(row_count, HEADS, HEAD_WIDTH)
    value_head_split = value_part.astype(jnp.float32).reshape(row_count, HEADS, HEAD_WIDTH)
    products = lax.optimization_barrier(jnp.sum(query_head_split * key_head_split, axis=-1, keepdims=True)) * HEAD_WIDTH ** (-0.5)
    return (jax.nn.silu(products) * value_head_split).reshape(row_count, HEADS * HEAD_WIDTH)

def history_rows(queries, key_rows, val_rows, length):
    query_count = queries.shape[0]
    key_count = key_rows.shape[0]
    query_head_split = queries.astype(jnp.float32).reshape(query_count, HEADS, HEAD_WIDTH)
    key_head_split = key_rows.astype(jnp.float32).reshape(key_count, HEADS, HEAD_WIDTH)
    value_head_split = val_rows.astype(jnp.float32).reshape(key_count, HEADS, HEAD_WIDTH)
    logit_scores = jnp.einsum('tgj,fgj->gtf', query_head_split, key_head_split) * HEAD_WIDTH ** (-0.5)
    inside = jnp.arange(key_count, dtype=jnp.int32) < length
    attention_weights = jnp.where(inside[None, None, :], jax.nn.silu(logit_scores), 0.0).astype(jnp.bfloat16)
    summed_output = jnp.einsum('fvc,cfj->vfj', attention_weights.astype(jnp.float32), value_head_split)
    return summed_output.reshape(query_count, HEADS * HEAD_WIDTH)

def reference(cand_rows, cand_col, w_in, w_out, hist_keys, hist_vals, hist_len):
    normed = layer_rows(cand_rows.astype(jnp.float32)).astype(jnp.bfloat16)
    projected = jax.nn.silu(jnp.dot(normed, w_in, preferred_element_type=jnp.float32)).astype(jnp.bfloat16)
    gate_part = projected[:, :D]
    value_part = projected[:, D:2 * D]
    query_part = projected[:, 2 * D:3 * D]
    key_part = projected[:, 3 * D:]
    self_term = self_scores(query_part, key_part, value_part)
    device_count = GROUPS * COLS
    by_device = cand_col.reshape(device_count, ROW_DEV)
    member = (by_device[:, :, None] == jnp.arange(COLS, dtype=jnp.int32)[None, None, :]).astype(jnp.int32)
    ranking = lax.optimization_barrier(jnp.sum((jnp.cumsum(member, axis=1) - member) * member, axis=2))
    device_ids = jnp.arange(device_count, dtype=jnp.int32)[:, None]
    user_ids = (device_ids // COLS * COLS + by_device).reshape(-1)
    slot_ids = (device_ids % COLS * MOST + ranking).reshape(-1)
    table = jnp.full((device_count, COLS * MOST), TOKENS, dtype=jnp.int32)
    table = table.at[user_ids, slot_ids].set(jnp.arange(TOKENS, dtype=jnp.int32))
    padded_queries = jnp.concatenate([query_part, jnp.zeros((1, D), query_part.dtype)], axis=0)
    flat_keys = hist_keys.reshape(device_count, HIST, D)
    flat_vals = hist_vals.reshape(device_count, HIST, D)
    flat_len = hist_len.reshape(device_count)

    def per_user(packed):
        indices, key_rows, val_rows, length = packed
        return history_rows(padded_queries[indices], key_rows, val_rows, length).astype(jnp.bfloat16)
    results = lax.map(per_user, (table, flat_keys, flat_vals, flat_len))
    history_term = jnp.zeros((TOKENS + 1, D), jnp.bfloat16).at[table.reshape(-1)].set(results.reshape(-1, D))[:TOKENS]
    attended = history_term.astype(jnp.float32) + self_term
    gated = (layer_rows(attended) * gate_part.astype(jnp.float32)).astype(jnp.bfloat16)
    output = jnp.dot(gated, w_out, preferred_element_type=jnp.float32) + cand_rows.astype(jnp.float32)
    return output.astype(jnp.bfloat16)
```

```python
import functools

import jax
import jax.numpy as jnp
from jax import lax
from jax.experimental import pallas as pl
from jax.experimental.pallas import tpu as pltpu
from jax.sharding import PartitionSpec as P

MESH = pl.DeviceIdType.MESH
F32 = jnp.float32
BF16 = jnp.bfloat16
D = 1024
HEAD = 64
MOST = 32
CW = 128
NCH = D // CW
EPS = 1e-05


def silu_of_half(half):
    return half + half * jnp.tanh(half)


def layer_rows(values):
    centred = values - jnp.mean(values, axis=-1, keepdims=True)
    variance = jnp.mean(centred * centred, axis=-1, keepdims=True)
    return centred / jnp.sqrt(variance + EPS)


def one_hots(col_row, rows, slots):
    r0 = lax.broadcasted_iota(jnp.int32, (rows, rows), 0)
    r1 = lax.broadcasted_iota(jnp.int32, (rows, rows), 1)
    col_wide = jnp.broadcast_to(col_row.astype(F32), (rows, rows))
    col = jnp.sum(jnp.where(r0 == r1, col_wide, 0.0), axis=1, keepdims=True)
    users = lax.broadcasted_iota(jnp.int32, (rows, 128), 1).astype(F32)
    member = jnp.where(users == col, 1.0, 0.0)
    before = jnp.where(r1 < r0, 1.0, 0.0).astype(BF16)
    count = jnp.dot(before, member.astype(BF16), preferred_element_type=F32)
    rank = jnp.sum(count * member, axis=1, keepdims=True)
    slot = col * MOST + rank
    slot_row = jnp.sum(jnp.where(r0 == r1, jnp.broadcast_to(slot, (rows, rows)), 0.0), axis=0, keepdims=True)
    lanes = lax.broadcasted_iota(jnp.int32, (rows, slots), 1).astype(F32)
    from_slot = jnp.where(lanes == slot, 1.0, 0.0).astype(BF16)
    subs = lax.broadcasted_iota(jnp.int32, (slots, rows), 0).astype(F32)
    to_slot = jnp.where(subs == slot_row, 1.0, 0.0).astype(BF16)
    return to_slot, from_slot


def kernel(
    ngrp, ndev,
    col_ref, len_ref, cand_ref, w_in_ref, w_out_ref, hk_ref, hv_ref, o_ref,
    kbuf, vbuf, qsend, qrecv, osend, oret, w_in, w_out, normed, proj, selft, att, to_slot, from_slot, acc,
    ksend_sem, krecv_sem, vsend_sem, vrecv_sem, qs_sem, qr_sem, os_sem, or_sem, w_sem,
):
    p = lax.axis_index("grp")
    d = lax.axis_index("dev")
    rows = cand_ref.shape[0]
    slots = ndev * MOST
    quarter = hk_ref.shape[2]
    others = slots - MOST

    order = (2, 3, 1, 0)
    w_copies = {}
    for i in order:
        w_copies[i] = pltpu.make_async_copy(w_in_ref.at[:, pl.ds(i * D, D)], w_in.at[i], w_sem.at[i])
        w_copies[i].start()
    w_out_copy = pltpu.make_async_copy(w_out_ref, w_out, w_sem.at[4])
    w_out_copy.start()

    barrier = pltpu.get_barrier_semaphore()

    def greet(i, carry):
        pl.semaphore_signal(barrier, inc=1, device_id=(p, lax.rem(d + i, ndev)), device_id_type=MESH)
        return carry

    for o in range(1, ngrp):
        pl.semaphore_signal(barrier, inc=1, device_id=(lax.rem(p + o, ngrp), d), device_id_type=MESH)
    lax.fori_loop(1, ndev, greet, 0)
    pl.semaphore_wait(barrier, ndev - 1 + ngrp - 1)

    def hist_copies(c, o):
        q = lax.rem(p + o, ngrp)
        cols = pl.ds(pl.multiple_of(c * CW, CW), CW)
        out = []
        for ref, buf, ss, rs in (
            (hk_ref, kbuf, ksend_sem, krecv_sem),
            (hv_ref, vbuf, vsend_sem, vrecv_sem),
        ):
            src = ref.at[q, 0, :, cols]
            dst = buf.at[c, p]
            if o == 0:
                out.append(pltpu.make_async_copy(src, dst, rs.at[c, 0]))
            else:
                out.append(
                    pltpu.make_async_remote_copy(
                        src_ref=src, dst_ref=dst, send_sem=ss.at[c, o], recv_sem=rs.at[c, o],
                        device_id=(q, d), device_id_type=MESH,
                    )
                )
        return out

    def send_hist(c, carry):
        for o in (1, 3, 2, 0):
            for copy in hist_copies(c, o):
                copy.start()
        return carry

    lax.fori_loop(0, NCH, send_hist, 0)

    first, second = one_hots(col_ref[...], rows, slots)
    to_slot[...] = first
    from_slot[...] = second
    normed[...] = layer_rows(cand_ref[...].astype(F32)).astype(BF16)

    def project(i):
        w_copies[i].wait()

        def part(j, carry):
            cols = pl.ds(pl.multiple_of(j * 256, 256), 256)
            half = jnp.dot(normed[...], w_in[i, :, cols], preferred_element_type=F32) * 0.5
            proj[i, :, cols] = silu_of_half(half).astype(BF16)
            return carry

        lax.fori_loop(0, D // 256, part, 0)

    project(2)

    def mine(src, dst, c):
        block = pl.ds(pl.multiple_of(d * MOST, MOST), MOST)
        dst[c, block, :] = src[c, block, :]

    def exchange(src, dst, ss, rs, c):
        def go(i, carry):
            e = lax.rem(d + i, ndev)
            pltpu.make_async_remote_copy(
                src_ref=src.at[c, pl.ds(pl.multiple_of(e * MOST, MOST), MOST)],
                dst_ref=dst.at[c, pl.ds(pl.multiple_of(d * MOST, MOST), MOST)],
                send_sem=ss.at[c], recv_sem=rs.at[c],
                device_id=(p, e), device_id_type=MESH,
            ).start()
            return carry

        lax.fori_loop(1, ndev, go, 0)

    def wait_all(buf, sem, c):
        view = buf.at[c, pl.ds(0, others)]
        pltpu.make_async_copy(view, view, sem.at[c]).wait()

    def dispatch(c, carry):
        cols = pl.ds(pl.multiple_of(c * CW, CW), CW)
        query = proj[2, :, cols] * jnp.bfloat16(HEAD**-0.5 * 0.5)
        qsend[c] = jnp.dot(to_slot[...], query, preferred_element_type=F32).astype(BF16)
        mine(qsend, qrecv, c)
        exchange(qsend, qrecv, qs_sem, qr_sem, c)
        return carry

    lax.fori_loop(0, NCH, dispatch, 0)

    project(3)
    project(1)
    project(0)

    head_a = lax.broadcasted_iota(jnp.int32, (CW, CW), 0) // HEAD
    head_b = lax.broadcasted_iota(jnp.int32, (CW, CW), 1) // HEAD
    same_head = jnp.where(head_a == head_b, 1.0, 0.0).astype(BF16)

    def self_part(c, carry):
        cols = pl.ds(pl.multiple_of(c * CW, CW), CW)
        product = proj[2, :, cols].astype(F32) * proj[3, :, cols].astype(F32)
        high = product.astype(BF16)
        low = (product - high.astype(F32)).astype(BF16)
        total = jnp.dot(high, same_head, preferred_element_type=F32) + jnp.dot(
            low, same_head, preferred_element_type=F32
        )
        selft[c] = silu_of_half(total * (HEAD**-0.5 * 0.5)) * proj[1, :, cols].astype(F32)
        return carry

    lax.fori_loop(0, NCH, self_part, 0)

    length = len_ref[p, 0]
    lane_head = lax.broadcasted_iota(jnp.int32, (quarter, CW), 1) // HEAD
    position = lax.broadcasted_iota(jnp.int32, (quarter, CW), 0)
    query_head = lax.broadcasted_iota(jnp.int32, (slots, CW), 1) // HEAD

    def gather(c):
        wait_all(oret, or_sem, c)
        history = jnp.dot(from_slot[...], oret[c], preferred_element_type=F32)
        att[c] = history + selft[c]

    def attend(c, carry):
        wait_all(qrecv, qr_sem, c)
        acc[...] = jnp.zeros_like(acc)
        for o in (0, 1, 3, 2):
            for copy in hist_copies(c, o):
                if o == 0:
                    copy.wait()
                else:
                    copy.wait_recv()
            src = lax.rem(p - o + ngrp, ngrp)
            keys = kbuf[c, src]
            vals = jnp.where(position + src * quarter < length, vbuf[c, src], jnp.bfloat16(0))
            total = None
            for h in range(CW // HEAD):
                query = jnp.where(query_head == h, qrecv[c], jnp.bfloat16(0))
                half = lax.dot_general(query, keys, (((1,), (1,)), ((), ())), preferred_element_type=F32)
                weights = silu_of_half(half).astype(BF16)
                head_vals = jnp.where(lane_head == h, vals, jnp.bfloat16(0))
                term = jnp.dot(weights, head_vals, preferred_element_type=F32)
                total = term if total is None else total + term
            acc[...] += total
        osend[c] = acc[...].astype(BF16)
        mine(osend, oret, c)
        exchange(osend, oret, os_sem, or_sem, c)
        return carry

    lax.fori_loop(0, NCH, attend, 0)

    for c in range(NCH):
        gather(c)

    attended = jnp.concatenate([att[c] for c in range(NCH)], axis=1)
    gated = (layer_rows(attended) * proj[0].astype(F32)).astype(BF16)
    w_out_copy.wait()
    o_ref[...] = (
        jnp.dot(gated, w_out[...], preferred_element_type=F32) + cand_ref[...].astype(F32)
    ).astype(BF16)

    def drain(c, carry):
        for o in range(1, ngrp):
            for copy in hist_copies(c, o):
                copy.wait_send()
        wait_all(qsend, qs_sem, c)
        wait_all(osend, os_sem, c)
        return carry

    lax.fori_loop(0, NCH, drain, 0)


def local(ngrp, ndev, cand_rows, cand_col, w_in, w_out, hist_keys, hist_vals, hist_len):
    rows = cand_rows.shape[0]
    slots = ndev * MOST
    quarter = hist_keys.shape[2]
    vmem = pl.BlockSpec(memory_space=pltpu.VMEM)
    hbm = pl.BlockSpec(memory_space=pl.ANY)
    smem = pl.BlockSpec(memory_space=pltpu.SMEM)
    dma = pltpu.SemaphoreType.DMA
    return pl.pallas_call(
        functools.partial(kernel, ngrp, ndev),
        out_shape=jax.ShapeDtypeStruct((rows, D), BF16),
        in_specs=[vmem, smem, vmem, hbm, hbm, hbm, hbm],
        out_specs=vmem,
        scratch_shapes=[
            pltpu.VMEM((NCH, ngrp, quarter, CW), BF16),
            pltpu.VMEM((NCH, ngrp, quarter, CW), BF16),
            pltpu.VMEM((NCH, slots, CW), BF16),
            pltpu.VMEM((NCH, slots, CW), BF16),
            pltpu.VMEM((NCH, slots, CW), BF16),
            pltpu.VMEM((NCH, slots, CW), BF16),
            pltpu.VMEM((4, D, D), BF16),
            pltpu.VMEM((D, D), BF16),
            pltpu.VMEM((rows, D), BF16),
            pltpu.VMEM((4, rows, D), BF16),
            pltpu.VMEM((NCH, rows, CW), F32),
            pltpu.VMEM((NCH, rows, CW), F32),
            pltpu.VMEM((slots, rows), BF16),
            pltpu.VMEM((rows, slots), BF16),
            pltpu.VMEM((slots, CW), F32),
            dma((NCH, ngrp)),
            dma((NCH, ngrp)),
            dma((NCH, ngrp)),
            dma((NCH, ngrp)),
            dma((NCH,)),
            dma((NCH,)),
            dma((NCH,)),
            dma((NCH,)),
            dma((5,)),
        ],
        compiler_params=pltpu.CompilerParams(
            collective_id=1, has_side_effects=True, vmem_limit_bytes=56 * 2**20
        ),
        cost_estimate=pl.CostEstimate(
            flops=2 * rows * 5 * D * D + 4 * slots * ngrp * quarter * D,
            bytes_accessed=24 * 2**20,
            transcendentals=slots * ngrp * quarter * D // HEAD,
        ),
    )(cand_col.reshape(1, rows), hist_len, cand_rows, w_in, w_out, hist_keys, hist_vals)


def solution(mesh):
    in_specs = (
        P(("grp", "dev"), None),
        P(("grp", "dev")),
        P(),
        P(),
        P(None, "dev", "grp", None),
        P(None, "dev", "grp", None),
        P(None, "dev"),
    )
    out_specs = P(("grp", "dev"), None)
    body = functools.partial(local, mesh.shape["grp"], mesh.shape["dev"])
    return jax.shard_map(body, mesh=mesh, in_specs=in_specs, out_specs=out_specs, check_vma=False)
```

```python
import functools

import jax
import jax.numpy as jnp
from jax import lax
from jax.experimental import pallas as pl
from jax.experimental.pallas import tpu as pltpu
from jax.sharding import PartitionSpec as P

MESH = pl.DeviceIdType.MESH
F32 = jnp.float32
BF16 = jnp.bfloat16
D = 1024
HEAD = 64
MOST = 32
CW = 128
NCH = D // CW
NPAIR = 4
EPS = 1e-05


def silu_of_half(half):
    return half + half * jnp.tanh(half)


def layer_rows(values):
    centred = values - jnp.mean(values, axis=-1, keepdims=True)
    variance = jnp.mean(centred * centred, axis=-1, keepdims=True)
    return centred / jnp.sqrt(variance + EPS)


def one_hots(col_row, rows, slots):
    r0 = lax.broadcasted_iota(jnp.int32, (rows, rows), 0)
    r1 = lax.broadcasted_iota(jnp.int32, (rows, rows), 1)
    col_wide = jnp.broadcast_to(col_row.astype(F32), (rows, rows))
    col = jnp.sum(jnp.where(r0 == r1, col_wide, 0.0), axis=1, keepdims=True)
    users = lax.broadcasted_iota(jnp.int32, (rows, 128), 1).astype(F32)
    member = jnp.where(users == col, 1.0, 0.0)
    before = jnp.where(r1 < r0, 1.0, 0.0).astype(BF16)
    count = jnp.dot(before, member.astype(BF16), preferred_element_type=F32)
    rank = jnp.sum(count * member, axis=1, keepdims=True)
    slot = col * MOST + rank
    slot_row = jnp.sum(jnp.where(r0 == r1, jnp.broadcast_to(slot, (rows, rows)), 0.0), axis=0, keepdims=True)
    lanes = lax.broadcasted_iota(jnp.int32, (rows, slots), 1).astype(F32)
    from_slot = jnp.where(lanes == slot, 1.0, 0.0).astype(BF16)
    subs = lax.broadcasted_iota(jnp.int32, (slots, rows), 0).astype(F32)
    to_slot = jnp.where(subs == slot_row, 1.0, 0.0).astype(BF16)
    return to_slot, from_slot


def kernel(
    ngrp, ndev,
    col_ref, len_ref, cand_ref, w_in_ref, w_out_ref, hk_ref, hv_ref, o_ref,
    kbuf, vbuf, qsend, qrecv, osend, oret, w_in, w_out, normed, proj, selft, att, to_slot, from_slot, acc,
    colbuf, rq_send, rq_recv, gq_send, gq_recv, go_send, go_ret, rr_send, rr_recv,
    ksend_sem, krecv_sem, vsend_sem, vrecv_sem, q_sem, o_sem, w_sem, col_sem, rq_sem, gq_sem, go_sem, rr_sem,
):
    p = lax.axis_index("grp")
    d = lax.axis_index("dev")
    rows = cand_ref.shape[0]
    slots = ndev * MOST
    quarter = hk_ref.shape[2]
    others = slots - MOST

    order = (2, 3, 1, 0)
    w_copies = {}
    for i in order:
        w_copies[i] = pltpu.make_async_copy(w_in_ref.at[:, pl.ds(i * D, D)], w_in.at[i], w_sem.at[i])
        w_copies[i].start()
    w_out_copy = pltpu.make_async_copy(w_out_ref, w_out, w_sem.at[4])
    w_out_copy.start()

    barrier = pltpu.get_barrier_semaphore()

    def greet(i, carry):
        pl.semaphore_signal(barrier, inc=1, device_id=(p, lax.rem(d + i, ndev)), device_id_type=MESH)
        return carry

    for o in range(1, ngrp):
        pl.semaphore_signal(barrier, inc=1, device_id=(lax.rem(p + o, ngrp), d), device_id_type=MESH)
    lax.fori_loop(1, ndev, greet, 0)
    pl.semaphore_wait(barrier, ndev - 1 + ngrp - 1)

    def remote(src, dst, send_sem, recv_sem, plane, dev):
        return pltpu.make_async_remote_copy(
            src_ref=src, dst_ref=dst, send_sem=send_sem, recv_sem=recv_sem,
            device_id=(plane, dev), device_id_type=MESH,
        )

    def arrived(view, sem):
        pltpu.make_async_copy(view, view, sem).wait()

    def plane_at(offset):
        return lax.rem(p + offset + ngrp, ngrp)

    def sign_of(s):
        return 1 - 2 * lax.rem(p + s, 2)

    def hist_copies(c, pieces):
        cols = pl.ds(pl.multiple_of(c * CW, CW), CW)
        out = []
        for group, plane, slot, sem in pieces:
            for ref, buf, ss, rs in (
                (hk_ref, kbuf, ksend_sem, krecv_sem),
                (hv_ref, vbuf, vsend_sem, vrecv_sem),
            ):
                src = ref.at[group, 0, :, cols]
                dst = buf.at[c, slot]
                if plane is None:
                    out.append(pltpu.make_async_copy(src, dst, rs.at[c, sem]))
                else:
                    out.append(remote(src, dst, ss.at[c, sem], rs.at[c, sem], plane, d))
        return out

    def home_pieces():
        return [(plane_at(o), plane_at(o), p, o) for o in (1, 3, 2)]

    def pair_pieces(s):
        sign = sign_of(s)
        return [(plane_at(sign), plane_at(sign), 1, 1), (plane_at(2), plane_at(sign), 3, 3)]

    def send_home(c):
        for copy in hist_copies(c, home_pieces() + [(p, None, p, 0)]):
            copy.start()

    def send_pair(c, s):
        own = [(p, None, 0, 0), (plane_at(-sign_of(s)), None, 2, 2)]
        for copy in hist_copies(c, pair_pieces(s) + own):
            copy.start()

    col_copies = [
        remote(col_ref, colbuf.at[s], col_sem.at[0, s], col_sem.at[1, s], plane_at(-sign_of(s)), d) for s in range(2)
    ]
    for copy in col_copies:
        copy.start()
    send_home(0)

    def slots_of(i, col_row):
        first, second = one_hots(col_row, rows, slots)
        to_slot[i] = first
        from_slot[i] = second

    slots_of(0, col_ref[...])
    normed[...] = layer_rows(cand_ref[...].astype(F32)).astype(BF16)

    def project(i):
        w_copies[i].wait()

        def part(j, carry):
            cols = pl.ds(pl.multiple_of(j * 256, 256), 256)
            half = jnp.dot(normed[...], w_in[i, :, cols], preferred_element_type=F32) * 0.5
            proj[i, :, cols] = silu_of_half(half).astype(BF16)
            return carry

        lax.fori_loop(0, D // 256, part, 0)

    project(2)

    def scaled_query(c):
        return proj[2, :, pl.ds(pl.multiple_of(c * CW, CW), CW)] * jnp.bfloat16(HEAD**-0.5 * 0.5)

    def rows_out(u):
        s = lax.rem(u, 2)
        return remote(rq_send.at[u], rq_recv.at[u], rq_sem.at[0, u], rq_sem.at[1, u], plane_at(-sign_of(s)), d)

    def results_out(u):
        s = lax.rem(u, 2)
        return remote(rr_send.at[u], rr_recv.at[u], rr_sem.at[0, u], rr_sem.at[1, u], plane_at(-sign_of(s)), d)

    def send_rows(u, carry):
        rq_send[u] = scaled_query(u + 1)
        rows_out(u).start()
        return carry

    lax.fori_loop(0, NPAIR, send_rows, 0)

    def send_pairs(u, carry):
        send_pair(u + 1, lax.rem(u, 2))
        return carry

    lax.fori_loop(0, NPAIR, send_pairs, 0)

    def exchange(src, dst, sems, c):
        block = pl.ds(pl.multiple_of(d * MOST, MOST), MOST)
        dst[c, block, :] = src[c, block, :]

        def go(i, carry):
            e = lax.rem(d + i, ndev)
            there = pl.ds(pl.multiple_of(e * MOST, MOST), MOST)
            remote(src.at[c, there], dst.at[c, block], sems.at[0, c], sems.at[1, c], p, e).start()
            return carry

        lax.fori_loop(1, ndev, go, 0)

    def exchange_sent(src, sems, c):
        arrived(src.at[c, pl.ds(0, others)], sems.at[0, c])

    def exchange_arrived(dst, sems, c):
        arrived(dst.at[c, pl.ds(0, others)], sems.at[1, c])

    def dispatch(c, carry):
        qsend[c] = jnp.dot(to_slot[0], scaled_query(c), preferred_element_type=F32).astype(BF16)
        exchange(qsend, qrecv, q_sem, c)
        return carry

    def dispatch_guest(u, carry):
        s = lax.rem(u, 2)
        rows_out(u).wait_recv()
        gq_send[u] = jnp.dot(to_slot[1 + s], rq_recv[u], preferred_element_type=F32).astype(BF16)
        exchange(gq_send, gq_recv, gq_sem, u)
        return carry

    lax.fori_loop(0, NPAIR + 1, dispatch, 0)
    for s in range(2):
        col_copies[s].wait_recv()
        slots_of(1 + s, colbuf[s])
    project(3)
    lax.fori_loop(0, NPAIR, dispatch_guest, 0)
    send_home(NPAIR + 1)
    lax.fori_loop(NPAIR + 1, NCH, dispatch, 0)

    project(1)
    project(0)

    head_a = lax.broadcasted_iota(jnp.int32, (CW, CW), 0) // HEAD
    head_b = lax.broadcasted_iota(jnp.int32, (CW, CW), 1) // HEAD
    same_head = jnp.where(head_a == head_b, 1.0, 0.0).astype(BF16)

    def self_part(c, carry):
        cols = pl.ds(pl.multiple_of(c * CW, CW), CW)
        product = proj[2, :, cols].astype(F32) * proj[3, :, cols].astype(F32)
        high = product.astype(BF16)
        low = (product - high.astype(F32)).astype(BF16)
        total = jnp.dot(high, same_head, preferred_element_type=F32) + jnp.dot(
            low, same_head, preferred_element_type=F32
        )
        selft[c] = silu_of_half(total * (HEAD**-0.5 * 0.5)) * proj[1, :, cols].astype(F32)
        return carry

    lax.fori_loop(0, NCH, self_part, 0)

    group = lax.broadcasted_iota(jnp.int32, (1, ngrp), 1)
    lane_head = lax.broadcasted_iota(jnp.int32, (quarter, CW), 1) // HEAD
    position = lax.broadcasted_iota(jnp.int32, (quarter, CW), 0)
    query_head = lax.broadcasted_iota(jnp.int32, (slots, CW), 1) // HEAD

    def attend(c, queries, out, i, parts, piece, user_group):
        length = jnp.sum(jnp.where(group == user_group, len_ref[...], 0), axis=1, keepdims=True)
        acc[...] = jnp.zeros_like(acc)

        def one(j, carry):
            sem, slot, src = piece(j)
            arrived(kbuf.at[c, slot], krecv_sem.at[c, sem])
            arrived(vbuf.at[c, slot], vrecv_sem.at[c, sem])
            keys = kbuf[c, slot]
            vals = jnp.where(position + src * quarter < length, vbuf[c, slot], jnp.bfloat16(0))
            total = None
            for h in range(CW // HEAD):
                query = jnp.where(query_head == h, queries[i], jnp.bfloat16(0))
                half = lax.dot_general(query, keys, (((1,), (1,)), ((), ())), preferred_element_type=F32)
                weights = silu_of_half(half).astype(BF16)
                head_vals = jnp.where(lane_head == h, vals, jnp.bfloat16(0))
                term = jnp.dot(weights, head_vals, preferred_element_type=F32)
                total = term if total is None else total + term
            acc[...] += total
            return carry

        lax.fori_loop(0, parts, one, 0)
        out[i] = acc[...].astype(BF16)

    def attend_home(c):
        def piece(j):
            o = lax.bitwise_xor(j, j // 2)
            src = plane_at(-o)
            return o, src, src

        exchange_arrived(qrecv, q_sem, c)
        attend(c, qrecv, osend, c, ngrp, piece, p)
        exchange(osend, oret, o_sem, c)

    def attend_pair(u):
        s = lax.rem(u, 2)
        sign = sign_of(s)
        exchange_arrived(qrecv, q_sem, u + 1)
        attend(u + 1, qrecv, osend, u + 1, 2, lambda j: (j, j, plane_at(sign * j)), p)
        exchange(osend, oret, o_sem, u + 1)
        exchange_arrived(gq_recv, gq_sem, u)
        attend(u + 1, gq_recv, go_send, u, 2, lambda j: (j + 2, j + 2, plane_at(sign * j)), plane_at(-sign))
        exchange(go_send, go_ret, go_sem, u)

    def gather_guest(u, carry):
        s = lax.rem(u, 2)
        exchange_arrived(go_ret, go_sem, u)
        rr_send[u] = jnp.dot(from_slot[1 + s], go_ret[u], preferred_element_type=F32).astype(BF16)
        results_out(u).start()
        return carry

    def gather(c):
        exchange_arrived(oret, o_sem, c)
        att[c] = jnp.dot(from_slot[0], oret[c], preferred_element_type=F32) + selft[c]

    def gather_pair(u, carry):
        results_out(u).wait()
        gather(u + 1)
        att[u + 1] += rr_recv[u].astype(F32)
        return carry

    def sent_home(c):
        for copy in hist_copies(c, home_pieces()):
            copy.wait_send()
        exchange_sent(qsend, q_sem, c)
        exchange_sent(osend, o_sem, c)

    def sent_pair(u, carry):
        for copy in hist_copies(u + 1, pair_pieces(lax.rem(u, 2))):
            copy.wait_send()
        exchange_sent(qsend, q_sem, u + 1)
        exchange_sent(osend, o_sem, u + 1)
        exchange_sent(gq_send, gq_sem, u)
        exchange_sent(go_send, go_sem, u)
        rows_out(u).wait_send()
        return carry

    attend_home(0)

    def pair_step(u, carry):
        @pl.when(NPAIR + 2 + u < NCH)
        def _():
            send_home(NPAIR + 2 + u)

        attend_pair(u)
        return carry

    lax.fori_loop(0, NPAIR, pair_step, 0)
    gather(0)
    sent_home(0)

    def step(c, carry):
        @pl.when((c + 3 < NCH) & (c + 3 > 2 * NPAIR + 1))
        def _():
            send_home(c + 3)

        attend_home(c)

        @pl.when(c == NPAIR + 1)
        def _():
            lax.fori_loop(0, NPAIR, gather_guest, 0)

        @pl.when(c > NPAIR + 1)
        def _():
            gather(c - 1)
            sent_home(c - 1)

        return carry

    lax.fori_loop(NPAIR + 1, NCH, step, 0)
    lax.fori_loop(0, NPAIR, sent_pair, 0)
    for copy in col_copies:
        copy.wait_send()
    sent_home(NCH - 1)
    lax.fori_loop(0, NPAIR, gather_pair, 0)
    gather(NCH - 1)

    attended = jnp.concatenate([att[c] for c in range(NCH)], axis=1)
    gated = (layer_rows(attended) * proj[0].astype(F32)).astype(BF16)
    w_out_copy.wait()
    o_ref[...] = (
        jnp.dot(gated, w_out[...], preferred_element_type=F32) + cand_ref[...].astype(F32)
    ).astype(BF16)


def local(ngrp, ndev, cand_rows, cand_col, w_in, w_out, hist_keys, hist_vals, hist_len):
    rows = cand_rows.shape[0]
    slots = ndev * MOST
    quarter = hist_keys.shape[2]
    vmem = pl.BlockSpec(memory_space=pltpu.VMEM)
    hbm = pl.BlockSpec(memory_space=pl.ANY)
    dma = pltpu.SemaphoreType.DMA
    return pl.pallas_call(
        functools.partial(kernel, ngrp, ndev),
        out_shape=jax.ShapeDtypeStruct((rows, D), BF16),
        in_specs=[vmem, vmem, vmem, hbm, hbm, hbm, hbm],
        out_specs=vmem,
        scratch_shapes=[
            pltpu.VMEM((NCH, ngrp, quarter, CW), BF16),
            pltpu.VMEM((NCH, ngrp, quarter, CW), BF16),
            pltpu.VMEM((NCH, slots, CW), BF16),
            pltpu.VMEM((NCH, slots, CW), BF16),
            pltpu.VMEM((NCH, slots, CW), BF16),
            pltpu.VMEM((NCH, slots, CW), BF16),
            pltpu.VMEM((4, D, D), BF16),
            pltpu.VMEM((D, D), BF16),
            pltpu.VMEM((rows, D), BF16),
            pltpu.VMEM((4, rows, D), BF16),
            pltpu.VMEM((NCH, rows, CW), F32),
            pltpu.VMEM((NCH, rows, CW), F32),
            pltpu.VMEM((3, slots, rows), BF16),
            pltpu.VMEM((3, rows, slots), BF16),
            pltpu.VMEM((slots, CW), F32),
            pltpu.VMEM((2, 1, rows), jnp.int32),
            pltpu.VMEM((NPAIR, rows, CW), BF16),
            pltpu.VMEM((NPAIR, rows, CW), BF16),
            pltpu.VMEM((NPAIR, slots, CW), BF16),
            pltpu.VMEM((NPAIR, slots, CW), BF16),
            pltpu.VMEM((NPAIR, slots, CW), BF16),
            pltpu.VMEM((NPAIR, slots, CW), BF16),
            pltpu.VMEM((NPAIR, rows, CW), BF16),
            pltpu.VMEM((NPAIR, rows, CW), BF16),
            dma((NCH, ngrp)),
            dma((NCH, ngrp)),
            dma((NCH, ngrp)),
            dma((NCH, ngrp)),
            dma((2, NCH)),
            dma((2, NCH)),
            dma((5,)),
            dma((2, 2)),
            dma((2, NPAIR)),
            dma((2, NPAIR)),
            dma((2, NPAIR)),
            dma((2, NPAIR)),
        ],
        compiler_params=pltpu.CompilerParams(
            collective_id=1, has_side_effects=True, vmem_limit_bytes=56 * 2**20
        ),
        cost_estimate=pl.CostEstimate(
            flops=2 * rows * 5 * D * D + 4 * slots * ngrp * quarter * D,
            bytes_accessed=24 * 2**20,
            transcendentals=slots * ngrp * quarter * D // HEAD,
        ),
    )(cand_col.reshape(1, rows), hist_len.reshape(1, ngrp), cand_rows, w_in, w_out, hist_keys, hist_vals)


def solution(mesh):
    in_specs = (
        P(("grp", "dev"), None),
        P(("grp", "dev")),
        P(),
        P(),
        P(None, "dev", "grp", None),
        P(None, "dev", "grp", None),
        P(None, "dev"),
    )
    out_specs = P(("grp", "dev"), None)
    body = functools.partial(local, mesh.shape["grp"], mesh.shape["dev"])
    return jax.shard_map(body, mesh=mesh, in_specs=in_specs, out_specs=out_specs, check_vma=False)
```

```python
import functools

import jax
import jax.numpy as jnp
from jax import lax
from jax.experimental import pallas as pl
from jax.experimental.pallas import tpu as pltpu
from jax.sharding import PartitionSpec as P

MESH = pl.DeviceIdType.MESH
F32 = jnp.float32
BF16 = jnp.bfloat16
D = 1024
HEAD = 64
MOST = 32
CW = 128
NCH = D // CW
NPAIR = 4
EPS = 1e-05


def silu_of_half(half):
    return half + half * jnp.tanh(half)


def layer_rows(values):
    centred = values - jnp.mean(values, axis=-1, keepdims=True)
    variance = jnp.mean(centred * centred, axis=-1, keepdims=True)
    return centred / jnp.sqrt(variance + EPS)


def one_hots(col_row, rows, slots):
    r0 = lax.broadcasted_iota(jnp.int32, (rows, rows), 0)
    r1 = lax.broadcasted_iota(jnp.int32, (rows, rows), 1)
    col_wide = jnp.broadcast_to(col_row.astype(F32), (rows, rows))
    col = jnp.sum(jnp.where(r0 == r1, col_wide, 0.0), axis=1, keepdims=True)
    users = lax.broadcasted_iota(jnp.int32, (rows, 128), 1).astype(F32)
    member = jnp.where(users == col, 1.0, 0.0)
    before = jnp.where(r1 < r0, 1.0, 0.0).astype(BF16)
    count = jnp.dot(before, member.astype(BF16), preferred_element_type=F32)
    rank = jnp.sum(count * member, axis=1, keepdims=True)
    slot = col * MOST + rank
    slot_row = jnp.sum(jnp.where(r0 == r1, jnp.broadcast_to(slot, (rows, rows)), 0.0), axis=0, keepdims=True)
    lanes = lax.broadcasted_iota(jnp.int32, (rows, slots), 1).astype(F32)
    from_slot = jnp.where(lanes == slot, 1.0, 0.0).astype(BF16)
    subs = lax.broadcasted_iota(jnp.int32, (slots, rows), 0).astype(F32)
    to_slot = jnp.where(subs == slot_row, 1.0, 0.0).astype(BF16)
    return to_slot, from_slot


def kernel(
    ngrp, ndev,
    col_ref, len_ref, cand_ref, w_in_ref, w_out_ref, hk_ref, hv_ref, o_ref,
    kbuf, vbuf, qsend, qrecv, osend, oret, w_in, w_out, normed, proj, selft, att, to_slot, from_slot, acc,
    colbuf, rq_send, rq_recv, gq_send, gq_recv, go_send, go_ret, rr_send, rr_recv,
    ksend_sem, krecv_sem, vsend_sem, vrecv_sem, q_sem, o_sem, w_sem, col_sem, rq_sem, gq_sem, go_sem, rr_sem, plane_sem,
):
    p = lax.axis_index("grp")
    d = lax.axis_index("dev")
    rows = cand_ref.shape[0]
    slots = ndev * MOST
    quarter = hk_ref.shape[2]
    others = slots - MOST

    order = (2, 3, 1, 0)
    w_copies = {}
    for i in order:
        w_copies[i] = pltpu.make_async_copy(w_in_ref.at[:, pl.ds(i * D, D)], w_in.at[i], w_sem.at[i])
        w_copies[i].start()
    w_out_copy = pltpu.make_async_copy(w_out_ref, w_out, w_sem.at[4])
    w_out_copy.start()

    barrier = pltpu.get_barrier_semaphore()

    odd = lax.rem(d, 2) == 1

    def greet(i, carry):
        e = 2 * i + 1

        @pl.when(e != d)
        def _():
            pl.semaphore_signal(barrier, inc=1, device_id=(p, e), device_id_type=MESH)

        return carry

    for o in range(1, ngrp):
        pl.semaphore_signal(barrier, inc=1, device_id=(lax.rem(p + o, ngrp), d), device_id_type=MESH)
    lax.fori_loop(0, ndev // 2, greet, 0)

    def remote(src, dst, send_sem, recv_sem, plane, dev):
        return pltpu.make_async_remote_copy(
            src_ref=src, dst_ref=dst, send_sem=send_sem, recv_sem=recv_sem,
            device_id=(plane, dev), device_id_type=MESH,
        )

    def arrived(view, sem):
        pltpu.make_async_copy(view, view, sem).wait()

    def plane_at(offset):
        return lax.rem(p + offset + ngrp, ngrp)

    def sign_of(s):
        return 1 - 2 * lax.rem(p + s, 2)

    def hist_copies(c, pieces):
        cols = pl.ds(pl.multiple_of(c * CW, CW), CW)
        out = []
        for group, plane, slot, sem in pieces:
            for ref, buf, ss, rs in (
                (hk_ref, kbuf, ksend_sem, krecv_sem),
                (hv_ref, vbuf, vsend_sem, vrecv_sem),
            ):
                src = ref.at[group, 0, :, cols]
                dst = buf.at[c, slot]
                if plane is None:
                    out.append(pltpu.make_async_copy(src, dst, rs.at[c, sem]))
                else:
                    out.append(remote(src, dst, ss.at[c, sem], rs.at[c, sem], plane, d))
        return out

    def home_pieces():
        return [(plane_at(o), plane_at(o), p, o) for o in (1, 3, 2)]

    def pair_pieces(s):
        sign = sign_of(s)
        return [(plane_at(sign), plane_at(sign), 1, 1), (plane_at(2), plane_at(sign), 3, 3)]

    def send_home(c):
        for copy in hist_copies(c, home_pieces() + [(p, None, p, 0)]):
            copy.start()

    def send_pair(c, s):
        own = [(p, None, 0, 0), (plane_at(-sign_of(s)), None, 2, 2)]
        for copy in hist_copies(c, pair_pieces(s) + own):
            copy.start()

    col_copies = [
        remote(col_ref, colbuf.at[s], col_sem.at[0, s], col_sem.at[1, s], plane_at(-sign_of(s)), d) for s in range(2)
    ]

    def slots_of(i, col_row):
        first, second = one_hots(col_row, rows, slots)
        to_slot[i] = first
        from_slot[i] = second

    slots_of(0, col_ref[...])

    @pl.when(odd)
    def _():
        pl.semaphore_wait(barrier, ndev - 1 + ngrp - 1)
        pl.semaphore_signal(plane_sem, inc=1, device_id=(p, d - 1), device_id_type=MESH)

    @pl.when(jnp.logical_not(odd))
    def _():
        pl.semaphore_wait(barrier, ngrp - 1)

    for copy in col_copies:
        copy.start()
    send_home(0)

    def project(i):
        w_copies[i].wait()

        def part(j, carry):
            cols = pl.ds(pl.multiple_of(j * 256, 256), 256)
            half = jnp.dot(normed[...], w_in[i, :, cols], preferred_element_type=F32) * 0.5
            proj[i, :, cols] = silu_of_half(half).astype(BF16)
            return carry

        lax.fori_loop(0, D // 256, part, 0)

    normed[...] = layer_rows(cand_ref[...].astype(F32)).astype(BF16)
    project(2)

    def scaled_query(c):
        return proj[2, :, pl.ds(pl.multiple_of(c * CW, CW), CW)] * jnp.bfloat16(HEAD**-0.5 * 0.5)

    def rows_out(u):
        s = lax.rem(u, 2)
        return remote(rq_send.at[u], rq_recv.at[u], rq_sem.at[0, u], rq_sem.at[1, u], plane_at(-sign_of(s)), d)

    def results_out(u):
        s = lax.rem(u, 2)
        return remote(rr_send.at[u], rr_recv.at[u], rr_sem.at[0, u], rr_sem.at[1, u], plane_at(-sign_of(s)), d)

    def send_rows(u, carry):
        rq_send[u] = scaled_query(u + 1)
        rows_out(u).start()
        return carry

    lax.fori_loop(0, NPAIR, send_rows, 0)

    def send_pairs(u, carry):
        send_pair(u + 1, lax.rem(u, 2))
        return carry

    lax.fori_loop(0, NPAIR, send_pairs, 0)

    def send_homes(c, carry):
        send_home(c)
        return carry

    lax.fori_loop(NPAIR + 1, NCH, send_homes, 0)

    def exchange(src, dst, sems, c):
        block = pl.ds(pl.multiple_of(d * MOST, MOST), MOST)
        dst[c, block, :] = src[c, block, :]

        def go(i, carry):
            e = lax.rem(d + i, ndev)
            there = pl.ds(pl.multiple_of(e * MOST, MOST), MOST)
            remote(src.at[c, there], dst.at[c, block], sems.at[0, c], sems.at[1, c], p, e).start()
            return carry

        lax.fori_loop(1, ndev, go, 0)

    def exchange_sent(src, sems, c):
        arrived(src.at[c, pl.ds(0, others)], sems.at[0, c])

    def exchange_arrived(dst, sems, c):
        arrived(dst.at[c, pl.ds(0, others)], sems.at[1, c])

    def dispatch(c, carry):
        qsend[c] = jnp.dot(to_slot[0], scaled_query(c), preferred_element_type=F32).astype(BF16)
        exchange(qsend, qrecv, q_sem, c)
        return carry

    def dispatch_guest(u, carry):
        s = lax.rem(u, 2)
        rows_out(u).wait_recv()
        gq_send[u] = jnp.dot(to_slot[1 + s], rq_recv[u], preferred_element_type=F32).astype(BF16)
        exchange(gq_send, gq_recv, gq_sem, u)
        return carry

    @pl.when(jnp.logical_not(odd))
    def _():
        pl.semaphore_wait(plane_sem, 1)

    lax.fori_loop(0, NPAIR + 1, dispatch, 0)
    for s in range(2):
        col_copies[s].wait_recv()
        slots_of(1 + s, colbuf[s])
    project(3)
    lax.fori_loop(0, NPAIR, dispatch_guest, 0)

    project(1)
    project(0)

    head_a = lax.broadcasted_iota(jnp.int32, (CW, CW), 0) // HEAD
    head_b = lax.broadcasted_iota(jnp.int32, (CW, CW), 1) // HEAD
    same_head = jnp.where(head_a == head_b, 1.0, 0.0).astype(BF16)

    def self_part(c, carry):
        cols = pl.ds(pl.multiple_of(c * CW, CW), CW)
        product = proj[2, :, cols].astype(F32) * proj[3, :, cols].astype(F32)
        high = product.astype(BF16)
        low = (product - high.astype(F32)).astype(BF16)
        total = jnp.dot(high, same_head, preferred_element_type=F32) + jnp.dot(
            low, same_head, preferred_element_type=F32
        )
        selft[c] = silu_of_half(total * (HEAD**-0.5 * 0.5)) * proj[1, :, cols].astype(F32)
        return carry

    lax.fori_loop(0, NCH, self_part, 0)

    group = lax.broadcasted_iota(jnp.int32, (1, ngrp), 1)
    lane_head = lax.broadcasted_iota(jnp.int32, (quarter, CW), 1) // HEAD
    position = lax.broadcasted_iota(jnp.int32, (quarter, CW), 0)
    query_head = lax.broadcasted_iota(jnp.int32, (slots, CW), 1) // HEAD

    def attend(c, queries, out, i, parts, piece, user_group):
        length = jnp.sum(jnp.where(group == user_group, len_ref[...], 0), axis=1, keepdims=True)
        acc[...] = jnp.zeros_like(acc)

        def one(j, carry):
            sem, slot, src = piece(j)
            arrived(kbuf.at[c, slot], krecv_sem.at[c, sem])
            arrived(vbuf.at[c, slot], vrecv_sem.at[c, sem])
            keys = kbuf[c, slot]
            vals = jnp.where(position + src * quarter < length, vbuf[c, slot], jnp.bfloat16(0))
            total = None
            for h in range(CW // HEAD):
                query = jnp.where(query_head == h, queries[i], jnp.bfloat16(0))
                half = lax.dot_general(query, keys, (((1,), (1,)), ((), ())), preferred_element_type=F32)
                weights = silu_of_half(half).astype(BF16)
                head_vals = jnp.where(lane_head == h, vals, jnp.bfloat16(0))
                term = jnp.dot(weights, head_vals, preferred_element_type=F32)
                total = term if total is None else total + term
            acc[...] += total
            return carry

        lax.fori_loop(0, parts, one, 0)
        out[i] = acc[...].astype(BF16)

    def attend_home(c):
        def piece(j):
            o = lax.bitwise_xor(j, j // 2)
            src = plane_at(-o)
            return o, src, src

        exchange_arrived(qrecv, q_sem, c)
        attend(c, qrecv, osend, c, ngrp, piece, p)
        exchange(osend, oret, o_sem, c)

    def attend_pair(u):
        s = lax.rem(u, 2)
        sign = sign_of(s)
        exchange_arrived(qrecv, q_sem, u + 1)
        attend(u + 1, qrecv, osend, u + 1, 2, lambda j: (j, j, plane_at(sign * j)), p)
        exchange(osend, oret, o_sem, u + 1)
        exchange_arrived(gq_recv, gq_sem, u)
        attend(u + 1, gq_recv, go_send, u, 2, lambda j: (j + 2, j + 2, plane_at(sign * j)), plane_at(-sign))
        exchange(go_send, go_ret, go_sem, u)

    def gather_guest(u):
        s = lax.rem(u, 2)
        exchange_arrived(go_ret, go_sem, u)
        rr_send[u] = jnp.dot(from_slot[1 + s], go_ret[u], preferred_element_type=F32).astype(BF16)
        results_out(u).start()

    def gather(c):
        exchange_arrived(oret, o_sem, c)
        att[c] = jnp.dot(from_slot[0], oret[c], preferred_element_type=F32) + selft[c]

    def gather_pair(u, carry):
        results_out(u).wait()
        gather(u + 1)
        att[u + 1] += rr_recv[u].astype(F32)
        return carry

    def sent_home(c):
        for copy in hist_copies(c, home_pieces()):
            copy.wait_send()
        exchange_sent(qsend, q_sem, c)
        exchange_sent(osend, o_sem, c)

    def sent_pair(u, carry):
        for copy in hist_copies(u + 1, pair_pieces(lax.rem(u, 2))):
            copy.wait_send()
        exchange_sent(qsend, q_sem, u + 1)
        exchange_sent(osend, o_sem, u + 1)
        exchange_sent(gq_send, gq_sem, u)
        exchange_sent(go_send, go_sem, u)
        rows_out(u).wait_send()
        return carry

    attend_home(0)

    def pair_step(u, carry):
        @pl.when(NPAIR + 1 + u < NCH)
        def _():
            dispatch(NPAIR + 1 + u, 0)

        attend_pair(u)

        @pl.when(u >= 2)
        def _():
            gather_guest(u - 2)

        return carry

    lax.fori_loop(0, NPAIR, pair_step, 0)

    def step(c, carry):
        @pl.when(c + NPAIR < NCH)
        def _():
            dispatch(c + NPAIR, 0)

        attend_home(c)

        @pl.when(c < NPAIR + 3)
        def _():
            gather_guest(c - 3)

        return carry

    lax.fori_loop(NPAIR + 1, NCH, step, 0)

    gather(0)
    sent_home(0)
    lax.fori_loop(0, NPAIR, sent_pair, 0)
    for copy in col_copies:
        copy.wait_send()

    def late(c, carry):
        gather(c)
        sent_home(c)
        return carry

    lax.fori_loop(NPAIR + 1, NCH - 1, late, 0)
    lax.fori_loop(0, NPAIR, gather_pair, 0)
    sent_home(NCH - 1)
    gather(NCH - 1)

    attended = jnp.concatenate([att[c] for c in range(NCH)], axis=1)
    gated = (layer_rows(attended) * proj[0].astype(F32)).astype(BF16)
    w_out_copy.wait()
    o_ref[...] = (
        jnp.dot(gated, w_out[...], preferred_element_type=F32) + cand_ref[...].astype(F32)
    ).astype(BF16)


def local(ngrp, ndev, cand_rows, cand_col, w_in, w_out, hist_keys, hist_vals, hist_len):
    rows = cand_rows.shape[0]
    slots = ndev * MOST
    quarter = hist_keys.shape[2]
    vmem = pl.BlockSpec(memory_space=pltpu.VMEM)
    hbm = pl.BlockSpec(memory_space=pl.ANY)
    dma = pltpu.SemaphoreType.DMA
    return pl.pallas_call(
        functools.partial(kernel, ngrp, ndev),
        out_shape=jax.ShapeDtypeStruct((rows, D), BF16),
        in_specs=[vmem, vmem, vmem, hbm, hbm, hbm, hbm],
        out_specs=vmem,
        scratch_shapes=[
            pltpu.VMEM((NCH, ngrp, quarter, CW), BF16),
            pltpu.VMEM((NCH, ngrp, quarter, CW), BF16),
            pltpu.VMEM((NCH, slots, CW), BF16),
            pltpu.VMEM((NCH, slots, CW), BF16),
            pltpu.VMEM((NCH, slots, CW), BF16),
            pltpu.VMEM((NCH, slots, CW), BF16),
            pltpu.VMEM((4, D, D), BF16),
            pltpu.VMEM((D, D), BF16),
            pltpu.VMEM((rows, D), BF16),
            pltpu.VMEM((4, rows, D), BF16),
            pltpu.VMEM((NCH, rows, CW), F32),
            pltpu.VMEM((NCH, rows, CW), F32),
            pltpu.VMEM((3, slots, rows), BF16),
            pltpu.VMEM((3, rows, slots), BF16),
            pltpu.VMEM((slots, CW), F32),
            pltpu.VMEM((2, 1, rows), jnp.int32),
            pltpu.VMEM((NPAIR, rows, CW), BF16),
            pltpu.VMEM((NPAIR, rows, CW), BF16),
            pltpu.VMEM((NPAIR, slots, CW), BF16),
            pltpu.VMEM((NPAIR, slots, CW), BF16),
            pltpu.VMEM((NPAIR, slots, CW), BF16),
            pltpu.VMEM((NPAIR, slots, CW), BF16),
            pltpu.VMEM((NPAIR, rows, CW), BF16),
            pltpu.VMEM((NPAIR, rows, CW), BF16),
            dma((NCH, ngrp)),
            dma((NCH, ngrp)),
            dma((NCH, ngrp)),
            dma((NCH, ngrp)),
            dma((2, NCH)),
            dma((2, NCH)),
            dma((5,)),
            dma((2, 2)),
            dma((2, NPAIR)),
            dma((2, NPAIR)),
            dma((2, NPAIR)),
            dma((2, NPAIR)),
            pltpu.SemaphoreType.REGULAR,
        ],
        compiler_params=pltpu.CompilerParams(
            collective_id=1, has_side_effects=True, vmem_limit_bytes=56 * 2**20
        ),
        cost_estimate=pl.CostEstimate(
            flops=2 * rows * 5 * D * D + 4 * slots * ngrp * quarter * D,
            bytes_accessed=24 * 2**20,
            transcendentals=slots * ngrp * quarter * D // HEAD,
        ),
    )(cand_col.reshape(1, rows), hist_len.reshape(1, ngrp), cand_rows, w_in, w_out, hist_keys, hist_vals)


def solution(mesh):
    in_specs = (
        P(("grp", "dev"), None),
        P(("grp", "dev")),
        P(),
        P(),
        P(None, "dev", "grp", None),
        P(None, "dev", "grp", None),
        P(None, "dev"),
    )
    out_specs = P(("grp", "dev"), None)
    body = functools.partial(local, mesh.shape["grp"], mesh.shape["dev"])
    return jax.shard_map(body, mesh=mesh, in_specs=in_specs, out_specs=out_specs, check_vma=False)
```

```python
import functools

import jax
import jax.numpy as jnp
from jax import lax
from jax.experimental import pallas as pl
from jax.experimental.pallas import tpu as pltpu
from jax.sharding import PartitionSpec as P

MESH = pl.DeviceIdType.MESH
F32 = jnp.float32
BF16 = jnp.bfloat16
D = 1024
HEAD = 64
MOST = 32
CW = 128
NCH = D // CW
HALVES = 2
NPAIR = 4
EPS = 1e-05


def silu_of_half(half):
    return half + half * jnp.tanh(half)


def layer_rows(values):
    centred = values - jnp.mean(values, axis=-1, keepdims=True)
    variance = jnp.mean(centred * centred, axis=-1, keepdims=True)
    return centred / jnp.sqrt(variance + EPS)


def one_hots(col_row, rows, slots):
    r0 = lax.broadcasted_iota(jnp.int32, (rows, rows), 0)
    r1 = lax.broadcasted_iota(jnp.int32, (rows, rows), 1)
    col_wide = jnp.broadcast_to(col_row.astype(F32), (rows, rows))
    col = jnp.sum(jnp.where(r0 == r1, col_wide, 0.0), axis=1, keepdims=True)
    users = lax.broadcasted_iota(jnp.int32, (rows, 128), 1).astype(F32)
    member = jnp.where(users == col, 1.0, 0.0)
    before = jnp.where(r1 < r0, 1.0, 0.0).astype(BF16)
    count = jnp.dot(before, member.astype(BF16), preferred_element_type=F32)
    rank = jnp.sum(count * member, axis=1, keepdims=True)
    slot = col * MOST + rank
    slot_row = jnp.sum(jnp.where(r0 == r1, jnp.broadcast_to(slot, (rows, rows)), 0.0), axis=0, keepdims=True)
    lanes = lax.broadcasted_iota(jnp.int32, (rows, slots), 1).astype(F32)
    from_slot = jnp.where(lanes == slot, 1.0, 0.0).astype(BF16)
    subs = lax.broadcasted_iota(jnp.int32, (slots, rows), 0).astype(F32)
    to_slot = jnp.where(subs == slot_row, 1.0, 0.0).astype(BF16)
    return to_slot, from_slot


def kernel(
    ngrp, ndev,
    col_ref, len_ref, cand_ref, w_in_ref, w_out_ref, hk_ref, hv_ref, o_ref,
    kbuf, vbuf, qsend, qrecv, osend, oret, w_in, w_out, normed, proj, selft, att, to_slot, from_slot, acc,
    colbuf, rq_send, rq_recv, gq_send, gq_recv, go_send, go_ret, rr_send, rr_recv,
    ksend_sem, krecv_sem, vsend_sem, vrecv_sem, q_sem, o_sem, w_sem, col_sem, rq_sem, gq_sem, go_sem, rr_sem, plane_sem,
):
    p = lax.axis_index("grp")
    d = lax.axis_index("dev")
    rows = cand_ref.shape[0]
    slots = ndev * MOST
    quarter = hk_ref.shape[2]
    others = slots - MOST

    order = (2, 3, 1, 0)
    w_copies = {}
    for i in order:
        w_copies[i] = pltpu.make_async_copy(w_in_ref.at[:, pl.ds(i * D, D)], w_in.at[i], w_sem.at[i])
        w_copies[i].start()
    w_out_copy = pltpu.make_async_copy(w_out_ref, w_out, w_sem.at[4])
    w_out_copy.start()

    barrier = pltpu.get_barrier_semaphore()

    odd = lax.rem(d, 2) == 1

    def greet(i, carry):
        e = 2 * i + 1

        @pl.when(e != d)
        def _():
            pl.semaphore_signal(barrier, inc=1, device_id=(p, e), device_id_type=MESH)

        return carry

    for o in range(1, ngrp):
        pl.semaphore_signal(barrier, inc=1, device_id=(lax.rem(p + o, ngrp), d), device_id_type=MESH)
    lax.fori_loop(0, ndev // 2, greet, 0)

    def remote(src, dst, send_sem, recv_sem, plane, dev):
        return pltpu.make_async_remote_copy(
            src_ref=src, dst_ref=dst, send_sem=send_sem, recv_sem=recv_sem,
            device_id=(plane, dev), device_id_type=MESH,
        )

    def arrived(view, sem):
        pltpu.make_async_copy(view, view, sem).wait()

    def plane_at(offset):
        return lax.rem(p + offset + ngrp, ngrp)

    def sign_of(s):
        return 1 - 2 * lax.rem(p + s, 2)

    def hist_copies(c, pieces):
        cols = pl.ds(pl.multiple_of(c * CW, CW), CW)
        out = []
        for group, plane, slot, sem in pieces:
            for ref, buf, ss, rs in (
                (hk_ref, kbuf, ksend_sem, krecv_sem),
                (hv_ref, vbuf, vsend_sem, vrecv_sem),
            ):
                src = ref.at[group, 0, :, cols]
                dst = buf.at[c, slot]
                if plane is None:
                    out.append(pltpu.make_async_copy(src, dst, rs.at[c, sem]))
                else:
                    out.append(remote(src, dst, ss.at[c, sem], rs.at[c, sem], plane, d))
        return out

    def home_pieces():
        return [(plane_at(o), plane_at(o), p, o) for o in (1, 3, 2)]

    def pair_pieces(s):
        sign = sign_of(s)
        return [(plane_at(sign), plane_at(sign), 1, 1), (plane_at(2), plane_at(sign), 3, 3)]

    def send_home(c):
        for copy in hist_copies(c, home_pieces() + [(p, None, p, 0)]):
            copy.start()

    def send_pair(c, s):
        own = [(p, None, 0, 0), (plane_at(-sign_of(s)), None, 2, 2)]
        for copy in hist_copies(c, pair_pieces(s) + own):
            copy.start()

    col_copies = [
        remote(col_ref, colbuf.at[s], col_sem.at[0, s], col_sem.at[1, s], plane_at(-sign_of(s)), d) for s in range(2)
    ]

    def slots_of(i, col_row):
        first, second = one_hots(col_row, rows, slots)
        to_slot[i] = first
        from_slot[i] = second

    def project(i):
        w_copies[i].wait()

        def part(j, carry):
            cols = pl.ds(pl.multiple_of(j * 256, 256), 256)
            half = jnp.dot(normed[...], w_in[i, :, cols], preferred_element_type=F32) * 0.5
            proj[i, :, cols] = silu_of_half(half).astype(BF16)
            return carry

        lax.fori_loop(0, D // 256, part, 0)

    def prepare():
        slots_of(0, col_ref[...])
        normed[...] = layer_rows(cand_ref[...].astype(F32)).astype(BF16)

    @pl.when(odd)
    def _():
        prepare()
        pl.semaphore_wait(barrier, ndev - 1 + ngrp - 1)
        pl.semaphore_signal(plane_sem, inc=1, device_id=(p, d - 1), device_id_type=MESH)

    @pl.when(jnp.logical_not(odd))
    def _():
        pl.semaphore_wait(barrier, ngrp - 1)

    for copy in col_copies:
        copy.start()
    send_home(0)

    @pl.when(jnp.logical_not(odd))
    def _():
        prepare()

    project(2)

    def scaled_query(c):
        return proj[2, :, pl.ds(pl.multiple_of(c * CW, CW), CW)] * jnp.bfloat16(HEAD**-0.5 * 0.5)

    def rows_out(u):
        s = lax.rem(u, 2)
        return remote(rq_send.at[u], rq_recv.at[u], rq_sem.at[0, u], rq_sem.at[1, u], plane_at(-sign_of(s)), d)

    def results_out(u):
        s = lax.rem(u, 2)
        return remote(rr_send.at[u], rr_recv.at[u], rr_sem.at[0, u], rr_sem.at[1, u], plane_at(-sign_of(s)), d)

    def send_rows(u, carry):
        rq_send[u] = scaled_query(u + 1)
        rows_out(u).start()
        return carry

    lax.fori_loop(0, NPAIR, send_rows, 0)
    send_pair(1, 0)

    def send_pairs(u, carry):
        send_pair(u + 1, lax.rem(u, 2))
        return carry

    def send_homes(c, carry):
        send_home(c)
        return carry

    def exchange(src, dst, sems, c):
        block = pl.ds(pl.multiple_of(d * MOST, MOST), MOST)
        dst[c, block, :] = src[c, block, :]

        def go(i, carry):
            e = lax.rem(d + i, ndev)
            there = pl.ds(pl.multiple_of(e * MOST, MOST), MOST)
            remote(src.at[c, there], dst.at[c, block], sems.at[0, c], sems.at[1, c], p, e).start()
            return carry

        lax.fori_loop(1, ndev, go, 0)

    def exchange_sent(src, sems, c):
        arrived(src.at[c, pl.ds(0, others)], sems.at[0, c])

    def exchange_arrived(dst, sems, c):
        arrived(dst.at[c, pl.ds(0, others)], sems.at[1, c])

    def dispatch(c, carry):
        qsend[c] = jnp.dot(to_slot[0], scaled_query(c), preferred_element_type=F32).astype(BF16)
        exchange(qsend, qrecv, q_sem, c)
        return carry

    def dispatch_guest(u, carry):
        s = lax.rem(u, 2)
        rows_out(u).wait_recv()
        gq_send[u] = jnp.dot(to_slot[1 + s], rq_recv[u], preferred_element_type=F32).astype(BF16)
        exchange(gq_send, gq_recv, gq_sem, u)
        return carry

    @pl.when(jnp.logical_not(odd))
    def _():
        pl.semaphore_wait(plane_sem, 1)

    dispatch(0, 0)
    lax.fori_loop(1, NPAIR, send_pairs, 0)
    lax.fori_loop(1, NPAIR + 1, dispatch, 0)
    lax.fori_loop(NPAIR + 1, NCH, send_homes, 0)
    for s in range(2):
        col_copies[s].wait_recv()
        slots_of(1 + s, colbuf[s])
    project(3)
    lax.fori_loop(0, NPAIR, dispatch_guest, 0)

    project(1)
    project(0)

    head_a = lax.broadcasted_iota(jnp.int32, (CW, CW), 0) // HEAD
    head_b = lax.broadcasted_iota(jnp.int32, (CW, CW), 1) // HEAD
    same_head = jnp.where(head_a == head_b, 1.0, 0.0).astype(BF16)

    def self_part(c, carry):
        cols = pl.ds(pl.multiple_of(c * CW, CW), CW)
        product = proj[2, :, cols].astype(F32) * proj[3, :, cols].astype(F32)
        high = product.astype(BF16)
        low = (product - high.astype(F32)).astype(BF16)
        total = jnp.dot(high, same_head, preferred_element_type=F32) + jnp.dot(
            low, same_head, preferred_element_type=F32
        )
        selft[c] = silu_of_half(total * (HEAD**-0.5 * 0.5)) * proj[1, :, cols].astype(F32)
        return carry

    lax.fori_loop(0, NCH, self_part, 0)

    group = lax.broadcasted_iota(jnp.int32, (1, ngrp), 1)
    lane_head = lax.broadcasted_iota(jnp.int32, (quarter, CW), 1) // HEAD
    position = lax.broadcasted_iota(jnp.int32, (quarter, CW), 0)

    def attend(c, queries, out, i, parts, piece, user_group, halves=None, send_block=None):
        length = jnp.sum(jnp.where(group == user_group, len_ref[...], 0), axis=1, keepdims=True)
        acc[...] = jnp.zeros_like(acc)

        def term_of(j, block):
            sem, slot, src = piece(j)
            keys = kbuf[c, slot]
            vals = jnp.where(position + src * quarter < length, vbuf[c, slot], jnp.bfloat16(0))
            total = None
            for h in range(CW // HEAD):
                query = queries[i, block, :]
                query_head = lax.broadcasted_iota(jnp.int32, query.shape, 1) // HEAD
                query = jnp.where(query_head == h, query, jnp.bfloat16(0))
                half = lax.dot_general(query, keys, (((1,), (1,)), ((), ())), preferred_element_type=F32)
                weights = silu_of_half(half).astype(BF16)
                head_vals = jnp.where(lane_head == h, vals, jnp.bfloat16(0))
                term = jnp.dot(weights, head_vals, preferred_element_type=F32)
                total = term if total is None else total + term
            return total

        def landed(j):
            sem, slot, src = piece(j)
            arrived(kbuf.at[c, slot], krecv_sem.at[c, sem])
            arrived(vbuf.at[c, slot], vrecv_sem.at[c, sem])

        def one(j, carry):
            landed(j)
            acc[...] += term_of(j, slice(None))
            return carry

        if halves is None:
            lax.fori_loop(0, parts, one, 0)
            out[i] = acc[...].astype(BF16)
        else:
            lax.fori_loop(0, parts - 1, one, 0)
            landed(parts - 1)
            size = slots // halves
            first = d // (ndev // halves)

            def part(k, carry):
                at = lax.rem(first + k, halves)
                block = pl.ds(pl.multiple_of(at * size, size), size)
                out[i, block, :] = (acc[block, :] + term_of(parts - 1, block)).astype(BF16)
                send_block(at * (ndev // halves))
                return carry

            lax.fori_loop(0, halves, part, 0)

    def attend_home(c, last=False):
        def piece(j):
            o = lax.bitwise_xor(j, j // 2)
            src = plane_at(-o)
            return o, src, src

        exchange_arrived(qrecv, q_sem, c)
        if not last:
            attend(c, qrecv, osend, c, ngrp, piece, p)
            exchange(osend, oret, o_sem, c)
            return

        mine = pl.ds(pl.multiple_of(d * MOST, MOST), MOST)

        def send_block(start):
            def go(k, carry):
                e = start + k
                there = pl.ds(pl.multiple_of(e * MOST, MOST), MOST)

                @pl.when(e != d)
                def _():
                    remote(osend.at[c, there], oret.at[c, mine], o_sem.at[0, c], o_sem.at[1, c], p, e).start()

                return carry

            lax.fori_loop(0, ndev // HALVES, go, 0)

        attend(c, qrecv, osend, c, ngrp, piece, p, HALVES, send_block)
        oret[c, mine, :] = osend[c, mine, :]

    def attend_pair(u):
        s = lax.rem(u, 2)
        sign = sign_of(s)
        exchange_arrived(qrecv, q_sem, u + 1)
        attend(u + 1, qrecv, osend, u + 1, 2, lambda j: (j, j, plane_at(sign * j)), p)
        exchange(osend, oret, o_sem, u + 1)
        exchange_arrived(gq_recv, gq_sem, u)
        attend(u + 1, gq_recv, go_send, u, 2, lambda j: (j + 2, j + 2, plane_at(sign * j)), plane_at(-sign))
        exchange(go_send, go_ret, go_sem, u)

    def gather_guest(u):
        s = lax.rem(u, 2)
        exchange_arrived(go_ret, go_sem, u)
        rr_send[u] = jnp.dot(from_slot[1 + s], go_ret[u], preferred_element_type=F32).astype(BF16)
        results_out(u).start()

    def gather(c):
        exchange_arrived(oret, o_sem, c)
        att[c] = jnp.dot(from_slot[0], oret[c], preferred_element_type=F32) + selft[c]

    def gather_pair(u, carry):
        results_out(u).wait()
        gather(u + 1)
        att[u + 1] += rr_recv[u].astype(F32)
        return carry

    def sent_home(c):
        for copy in hist_copies(c, home_pieces()):
            copy.wait_send()
        exchange_sent(qsend, q_sem, c)
        exchange_sent(osend, o_sem, c)

    def sent_pair(u, carry):
        for copy in hist_copies(u + 1, pair_pieces(lax.rem(u, 2))):
            copy.wait_send()
        exchange_sent(qsend, q_sem, u + 1)
        exchange_sent(osend, o_sem, u + 1)
        exchange_sent(gq_send, gq_sem, u)
        exchange_sent(go_send, go_sem, u)
        rows_out(u).wait_send()
        return carry

    attend_home(0)

    def pair_step(u, carry):
        @pl.when(NPAIR + 1 + u < NCH)
        def _():
            dispatch(NPAIR + 1 + u, 0)

        attend_pair(u)

        @pl.when(u >= 2)
        def _():
            gather_guest(u - 2)

        return carry

    lax.fori_loop(0, NPAIR, pair_step, 0)

    def step(c, carry):
        @pl.when(c + NPAIR < NCH)
        def _():
            dispatch(c + NPAIR, 0)

        attend_home(c)

        @pl.when(c < NPAIR + 3)
        def _():
            gather_guest(c - 3)

        return carry

    lax.fori_loop(NPAIR + 1, NCH - 1, step, 0)

    def late(c, carry):
        gather(c)
        sent_home(c)
        return carry

    late(0, 0)
    lax.fori_loop(0, NPAIR, sent_pair, 0)
    for copy in col_copies:
        copy.wait_send()
    lax.fori_loop(NPAIR + 1, NCH - 2, late, 0)
    attend_home(NCH - 1, last=True)

    late(NCH - 2, 0)
    lax.fori_loop(0, NPAIR, gather_pair, 0)
    sent_home(NCH - 1)

    def statistics(values):
        mean = jnp.mean(values, axis=-1, keepdims=True)
        centred = values - mean
        return mean, jnp.sum(centred * centred, axis=-1, keepdims=True)

    early_width = D - CW
    early_mean, early_square = statistics(jnp.concatenate([att[c] for c in range(NCH - 1)], axis=1))
    gather(NCH - 1)
    late_mean, late_square = statistics(att[NCH - 1])
    apart = late_mean - early_mean
    mean = early_mean + apart * (CW / D)
    variance = (early_square + late_square + apart * apart * (early_width * CW / D)) * (1.0 / D)
    deviation = jnp.sqrt(variance + EPS)
    attended = jnp.concatenate([att[c] for c in range(NCH)], axis=1)
    gated = ((attended - mean) / deviation * proj[0].astype(F32)).astype(BF16)
    w_out_copy.wait()
    o_ref[...] = (
        jnp.dot(gated, w_out[...], preferred_element_type=F32) + cand_ref[...].astype(F32)
    ).astype(BF16)


def local(ngrp, ndev, cand_rows, cand_col, w_in, w_out, hist_keys, hist_vals, hist_len):
    rows = cand_rows.shape[0]
    slots = ndev * MOST
    quarter = hist_keys.shape[2]
    vmem = pl.BlockSpec(memory_space=pltpu.VMEM)
    hbm = pl.BlockSpec(memory_space=pl.ANY)
    dma = pltpu.SemaphoreType.DMA
    return pl.pallas_call(
        functools.partial(kernel, ngrp, ndev),
        out_shape=jax.ShapeDtypeStruct((rows, D), BF16),
        in_specs=[vmem, vmem, vmem, hbm, hbm, hbm, hbm],
        out_specs=vmem,
        scratch_shapes=[
            pltpu.VMEM((NCH, ngrp, quarter, CW), BF16),
            pltpu.VMEM((NCH, ngrp, quarter, CW), BF16),
            pltpu.VMEM((NCH, slots, CW), BF16),
            pltpu.VMEM((NCH, slots, CW), BF16),
            pltpu.VMEM((NCH, slots, CW), BF16),
            pltpu.VMEM((NCH, slots, CW), BF16),
            pltpu.VMEM((4, D, D), BF16),
            pltpu.VMEM((D, D), BF16),
            pltpu.VMEM((rows, D), BF16),
            pltpu.VMEM((4, rows, D), BF16),
            pltpu.VMEM((NCH, rows, CW), F32),
            pltpu.VMEM((NCH, rows, CW), F32),
            pltpu.VMEM((3, slots, rows), BF16),
            pltpu.VMEM((3, rows, slots), BF16),
            pltpu.VMEM((slots, CW), F32),
            pltpu.VMEM((2, 1, rows), jnp.int32),
            pltpu.VMEM((NPAIR, rows, CW), BF16),
            pltpu.VMEM((NPAIR, rows, CW), BF16),
            pltpu.VMEM((NPAIR, slots, CW), BF16),
            pltpu.VMEM((NPAIR, slots, CW), BF16),
            pltpu.VMEM((NPAIR, slots, CW), BF16),
            pltpu.VMEM((NPAIR, slots, CW), BF16),
            pltpu.VMEM((NPAIR, rows, CW), BF16),
            pltpu.VMEM((NPAIR, rows, CW), BF16),
            dma((NCH, ngrp)),
            dma((NCH, ngrp)),
            dma((NCH, ngrp)),
            dma((NCH, ngrp)),
            dma((2, NCH)),
            dma((2, NCH)),
            dma((5,)),
            dma((2, 2)),
            dma((2, NPAIR)),
            dma((2, NPAIR)),
            dma((2, NPAIR)),
            dma((2, NPAIR)),
            pltpu.SemaphoreType.REGULAR,
        ],
        compiler_params=pltpu.CompilerParams(
            collective_id=1, has_side_effects=True, vmem_limit_bytes=56 * 2**20
        ),
        cost_estimate=pl.CostEstimate(
            flops=2 * rows * 5 * D * D + 4 * slots * ngrp * quarter * D,
            bytes_accessed=24 * 2**20,
            transcendentals=slots * ngrp * quarter * D // HEAD,
        ),
    )(cand_col.reshape(1, rows), hist_len.reshape(1, ngrp), cand_rows, w_in, w_out, hist_keys, hist_vals)


def solution(mesh):
    in_specs = (
        P(("grp", "dev"), None),
        P(("grp", "dev")),
        P(),
        P(),
        P(None, "dev", "grp", None),
        P(None, "dev", "grp", None),
        P(None, "dev"),
    )
    out_specs = P(("grp", "dev"), None)
    body = functools.partial(local, mesh.shape["grp"], mesh.shape["dev"])
    return jax.shard_map(body, mesh=mesh, in_specs=in_specs, out_specs=out_specs, check_vma=False)
```
